32 devices in a mesh: ctx: 8 (over z, y), kv: 4 (over x, core).
Axes of the slice: x: 2, y: 2, z: 4, core: 2. Of those that a mesh axis runs over, the one named last changes fastest.
Arguments:
- tokens: bfloat16 [4096, 8192], P('ctx', 'kv'), may hold values from -6 to 6
- segment_ids: int32 [4096], replicated, may hold values from 0 to 15, never falling along the last dimension, each value on 1 to 1024 neighbouring positions
- query_weight: bfloat16 [8192, 4096], P('ctx', 'kv'), may hold values from -2 to 2
- key_weight: bfloat16 [8192, 512], P('ctx', 'kv'), may hold values from -2 to 2
- value_projection_matrix: bfloat16 [8192, 512], P('ctx', 'kv'), may hold values from -0.0625 to 0.0625
Outputs:
- attended: bfloat16 [4096, 4096], P('ctx', 'kv')
The draws below stay inside these ranges and needn't reach their ends.
Inputs may be any that keep to these rules, and one draw needn't show every extreme that they name: `segment_ids`: segment ids never fall along the sequence; each document holds 1 to 1024 tokens and one holds exactly 1024.
All inputs are finite; a program needn't handle non-finite values.
Results may differ from the reference program's by a relative error of at most 0.0085.
Values may be sent and summed in bfloat16 or wider, within the bound.
A program may use at most 128 MiB of HBM per device.

```python
import math
import jax
import jax.numpy as jnp
import numpy as np
from jax import lax

MODEL_WIDTH = 8192
QUERY_HEADS = 32
KEY_VALUE_HEADS = 4
HEAD_DIMENSION = 128
TOKENS_PER_SHARD = 512
TOKENS = 4096
WINDOW = 512
N_CTX = 8


def draw_query_weight(key, part):
    baseline_jitter = jax.random.truncated_normal(jax.random.fold_in(key, 11), -6.0, 6.0, (MODEL_WIDTH, QUERY_HEADS * HEAD_DIMENSION), jnp.float32) * MODEL_WIDTH ** (-0.5)
    return baseline_jitter.astype(jnp.bfloat16)


def draw_key_weight(key, part):
    baseline_jitter = jax.random.truncated_normal(jax.random.fold_in(key, 12), -6.0, 6.0, (MODEL_WIDTH, KEY_VALUE_HEADS * HEAD_DIMENSION), jnp.float32) * MODEL_WIDTH ** (-0.5)
    return baseline_jitter.astype(jnp.bfloat16)


def levels(stream_key, extent, pieces, low, high):
    factor_of = 1.0
    for position, blocks in pieces:
        heights = jax.random.uniform(jax.random.fold_in(jax.random.fold_in(stream_key, 6), position), (blocks,), jnp.float32, low / len(pieces), high / len(pieces))
        factor_of = factor_of * jnp.repeat(jnp.exp(heights), extent[position] // blocks).reshape((-1,) + (1,) * (len(extent) - 1 - position))
    return factor_of


def split_up(number_of, total, most, lean):
    weights = [(1 << 20) // math.isqrt(grade ** lean) + 1 for grade in range(2, number_of + 1)]
    rest, holding = total - most - (number_of - 1), [1] * (number_of - 1)
    while rest > 0:
        free = [i for i in range(number_of - 1) if holding[i] < most]
        whole, remaining = sum([weights[i] for i in free]), rest
        for i in free:
            addition = min(most - holding[i], max(1, remaining * weights[i] // whole), rest)
            holding[i] = holding[i] + addition
            rest = rest - addition
    return np.array([most] + holding)


def uneven_parts(rng, number_of, total, limit, lean):
    if number_of == 2:
        one = jax.random.randint(rng, (), max(1, total - limit), min(limit, total - 1) + 1)
        return jnp.stack([one, total - one])
    lengths = jnp.asarray(split_up(number_of, total, limit, lean), jnp.int32)
    pairs = (number_of - 1) // 2
    giver, taker = lengths[1:1 + 2 * pairs:2], lengths[2:2 + 2 * pairs:2]
    slack = jnp.minimum(giver - 1, limit - taker)
    shifted = jax.random.randint(jax.random.fold_in(rng, 1), (pairs,), 0, 1 << 20) % (slack + 1)
    lengths = lengths.at[1:1 + 2 * pairs:2].set(giver - shifted).at[2:2 + 2 * pairs:2].set(taker + shifted)
    return lengths[jax.random.permutation(jax.random.fold_in(rng, 2), number_of)]


def bell_draw(rng, dims, scale, limit, cuts=(), kind=jnp.bfloat16):
    drawn = jax.random.normal(rng, dims, jnp.float32) * scale
    if len(cuts) > 0:
        drawn = levels(rng, dims, cuts, -0.22, 0.18) * drawn
    return jnp.clip(drawn, min=-limit, max=limit).astype(kind)


def setup_inputs(seed: int = 0) -> dict:
    streams_of = jax.random.split(jax.random.key(seed), 6)
    return {
        "tokens": bell_draw(streams_of[0], (TOKENS, MODEL_WIDTH), 1.0, 6.0, ((0, 8), (1, 4))),
        "segment_ids": jnp.searchsorted(jnp.cumsum(uneven_parts(streams_of[1], 2 * N_CTX, TOKENS, 2 * TOKENS_PER_SHARD, 1)), jnp.arange(TOKENS), side="right").astype(jnp.int32),
        "query_weight": draw_query_weight(jax.random.fold_in(streams_of[5], 71), 0),
        "key_weight": draw_key_weight(jax.random.fold_in(streams_of[5], 71), 0),
        "value_projection_matrix": bell_draw(streams_of[4], (MODEL_WIDTH, KEY_VALUE_HEADS * HEAD_DIMENSION), MODEL_WIDTH ** -0.5, 0.0625, ((0, 8), (1, 4))),
    }


def attend_block(query_matrix, key_matrix, value_matrix, visible):
    scores = jnp.einsum("thgd,shd->hgts", query_matrix.astype(jnp.float32), key_matrix.astype(jnp.float32)) * (HEAD_DIMENSION ** -0.5)
    scores = jnp.where(visible[None, None], scores, -1e30)
    largest = jnp.max(scores, axis=-1, keepdims=True)
    expon = jnp.where(visible[None, None], jnp.exp(scores - largest), 0.0)
    total = jnp.sum(expon, axis=-1, keepdims=True)
    weights = expon.astype(jnp.bfloat16)
    summed = jnp.einsum("hgts,shd->hgtd", weights.astype(jnp.float32), value_matrix.astype(jnp.float32))
    result = summed / total
    rows = query_matrix.shape[0]
    return jnp.transpose(result, (2, 0, 1, 3)).reshape(rows, -1).astype(jnp.bfloat16)


def reference(tokens, segment_ids, query_weight, key_weight, value_projection_matrix):
    query_group = QUERY_HEADS // KEY_VALUE_HEADS
    key_matrix = jnp.dot(tokens, key_weight, preferred_element_type=jnp.float32).astype(jnp.bfloat16)
    value_matrix = jnp.dot(tokens, value_projection_matrix, preferred_element_type=jnp.float32).astype(jnp.bfloat16)
    padded_keys = jnp.concatenate([jnp.zeros((TOKENS_PER_SHARD, KEY_VALUE_HEADS * HEAD_DIMENSION), jnp.bfloat16), key_matrix], axis=0)
    padded_values = jnp.concatenate([jnp.zeros((TOKENS_PER_SHARD, KEY_VALUE_HEADS * HEAD_DIMENSION), jnp.bfloat16), value_matrix], axis=0)
    seg_pad = jnp.concatenate([jnp.full((TOKENS_PER_SHARD,), -1, jnp.int32), segment_ids.astype(jnp.int32)], axis=0)

    def one_block(block):
        begin_offset = (block * TOKENS_PER_SHARD).astype(jnp.int32)
        rows_x = lax.dynamic_slice_in_dim(tokens, begin_offset, TOKENS_PER_SHARD, 0)
        query_matrix = jnp.dot(rows_x, query_weight, preferred_element_type=jnp.float32).astype(jnp.bfloat16)
        query_matrix = query_matrix.reshape(TOKENS_PER_SHARD, KEY_VALUE_HEADS, query_group, HEAD_DIMENSION)
        nearby_keys = lax.dynamic_slice_in_dim(padded_keys, begin_offset, 2 * TOKENS_PER_SHARD, 0).reshape(2 * TOKENS_PER_SHARD, KEY_VALUE_HEADS, HEAD_DIMENSION)
        nearby_values = lax.dynamic_slice_in_dim(padded_values, begin_offset, 2 * TOKENS_PER_SHARD, 0).reshape(2 * TOKENS_PER_SHARD, KEY_VALUE_HEADS, HEAD_DIMENSION)
        seg_query = lax.dynamic_slice_in_dim(segment_ids.astype(jnp.int32), begin_offset, TOKENS_PER_SHARD, 0)
        seg_keys = lax.dynamic_slice_in_dim(seg_pad, begin_offset, 2 * TOKENS_PER_SHARD, 0)
        qpos = begin_offset + jnp.arange(TOKENS_PER_SHARD, dtype=jnp.int32)
        kpos = begin_offset - TOKENS_PER_SHARD + jnp.arange(2 * TOKENS_PER_SHARD, dtype=jnp.int32)
        visible = (kpos[None, :] <= qpos[:, None]) & (kpos[None, :] > qpos[:, None] - WINDOW)
        visible = visible & (kpos[None, :] >= 0) & (seg_keys[None, :] == seg_query[:, None])
        return attend_block(query_matrix, nearby_keys, nearby_values, visible)

    blocks = lax.map(one_block, jnp.arange(TOKENS // TOKENS_PER_SHARD, dtype=jnp.int32))
    return blocks.reshape(TOKENS, QUERY_HEADS * HEAD_DIMENSION)
```

```python
import functools

import jax
import jax.numpy as jnp
from jax import lax
from jax.experimental import pallas as pl
from jax.experimental.pallas import tpu as pltpu
from jax.sharding import PartitionSpec as P

HEAD_DIMENSION = 128


def shifted(shard, axis, by):
    length = lax.axis_size(axis)
    pairs = [(i, i + by) for i in range(length) if 0 <= i + by < length]
    return lax.ppermute(shard, axis, pairs)


def attend_block(query_matrix, key_matrix, value_matrix, visible):
    head_size = query_matrix.shape[-1]
    scores = jnp.einsum(
        "thgd,shd->hgts", query_matrix, key_matrix, preferred_element_type=jnp.float32
    ) * head_size ** (-0.5)
    scores = jnp.where(visible[None, None], scores, -1e30)
    largest = jnp.max(scores, axis=-1, keepdims=True)
    expon = jnp.where(visible[None, None], jnp.exp(scores - largest), 0.0)
    total = jnp.sum(expon, axis=-1, keepdims=True)
    weights = expon.astype(jnp.bfloat16)
    summed = jnp.einsum("hgts,shd->hgtd", weights, value_matrix, preferred_element_type=jnp.float32)
    result = summed / total
    rows = query_matrix.shape[0]
    return jnp.transpose(result, (2, 0, 1, 3)).reshape(rows, -1).astype(jnp.bfloat16)


MESH = pl.DeviceIdType.MESH


def gather_kernel(lines, pieces, tok, wgt, tok_all, wgt_all, loc, tsend, trecv,
                  up_s, up_r, dn_s, dn_r, y_s, y_r):
    ctx, kv = lax.axis_index("ctx"), lax.axis_index("kv")
    z, y = ctx // 2, ctx % 2
    up, down, across = {"ctx": ctx + 2}, {"ctx": ctx - 2}, {"ctx": z * 2 + (1 - y)}
    core = {"kv": (kv // 2) * 2 + (1 - kv % 2)}
    far = {"kv": (1 - kv // 2) * 2 + kv % 2}
    has_up, has_down = z < lines - 1, z > 0
    height, depth = tok.shape[1], wgt.shape[0]
    rows = depth // pieces

    barrier = pltpu.get_barrier_semaphore()
    for other in (across, core, far):
        pl.semaphore_signal(barrier, inc=1, device_id=other, device_id_type=MESH)

    @pl.when(has_up)
    def _():
        pl.semaphore_signal(barrier, inc=1, device_id=up, device_id_type=MESH)

    @pl.when(has_down)
    def _():
        pl.semaphore_signal(barrier, inc=1, device_id=down, device_id_type=MESH)

    pl.semaphore_wait(barrier, 3 + has_up.astype(jnp.int32) + has_down.astype(jnp.int32))

    def copy(src, dst, send, recv, other):
        return pltpu.make_async_remote_copy(
            src_ref=src, dst_ref=dst, send_sem=send, recv_sem=recv,
            device_id=other, device_id_type=MESH)

    def place(line, side, p):
        start = pl.multiple_of((line * 2 + side) * depth + p * rows, rows)
        return wgt_all.at[pl.ds(start, rows), :]

    def block(off, p):
        return wgt.at[pl.ds(p * rows, rows), :] if off == 0 else place(z + off, y, p)

    def up_copy(d, p):
        return copy(block(-d, p), place(z - d, y, p), up_s.at[d, p], up_r.at[d, p], up)

    def down_copy(d, p):
        return copy(block(d, p), place(z + d, y, p), dn_s.at[d, p], dn_r.at[d, p], down)

    def y_copy(off, p):
        i = off + lines - 1
        return copy(block(off, p), place(z + off, y, p), y_s.at[i, p], y_r.at[i, p], across)

    def columns(k):
        return tok_all.at[:, pl.ds(pl.multiple_of(k * height, height), height)]

    for p in range(pieces):
        pl.when(has_up)(lambda p=p: up_copy(0, p).start())
        pl.when(has_down)(lambda p=p: down_copy(0, p).start())
        y_copy(0, p).start()
    other_core = core["kv"]
    own_far = copy(tok, columns(kv), tsend.at[0], trecv.at[0], far)
    own_core = copy(tok, columns(kv), tsend.at[1], trecv.at[1], core)
    pass_on = copy(columns(far["kv"]), columns(far["kv"]), tsend.at[2], trecv.at[2], core)
    own_far.start()
    own_core.start()
    local = [pltpu.make_async_copy(tok, columns(kv), loc.at[0]),
             pltpu.make_async_copy(
                 wgt, wgt_all.at[pl.ds(pl.multiple_of(ctx * depth, depth), depth), :], loc.at[1])]
    for c in local:
        c.start()

    for d in range(1, lines):
        for p in range(pieces):
            @pl.when(z >= d)
            def _(d=d, p=p):
                up_copy(d - 1, p).wait_recv()
                y_copy(-d, p).start()
                if d < lines - 1:
                    pl.when(has_up)(lambda: up_copy(d, p).start())

            @pl.when(z + d < lines)
            def _(d=d, p=p):
                down_copy(d - 1, p).wait_recv()
                y_copy(d, p).start()
                if d < lines - 1:
                    pl.when(has_down)(lambda: down_copy(d, p).start())
        if d == 1:
            own_far.wait_recv()
            pass_on.start()
    if lines == 1:
        own_far.wait_recv()
        pass_on.start()

    own_core.wait_recv()
    pass_on.wait_recv()
    for c in (own_far, own_core, pass_on):
        c.wait_send()
    for c in local:
        c.wait()
    for p in range(pieces):
        for d in range(lines):
            if d < lines - 1:
                pl.when(has_up & (z >= d))(lambda d=d, p=p: up_copy(d, p).wait_send())
                pl.when(has_down & (z + d < lines))(lambda d=d, p=p: down_copy(d, p).wait_send())
            pl.when(z >= d)(lambda d=d, p=p: y_copy(-d, p).wait())
            if d > 0:
                pl.when(z + d < lines)(lambda d=d, p=p: y_copy(d, p).wait())


def gathered(tokens, weights):
    lines = lax.axis_size("ctx") // 2
    depth, width = weights.shape
    pieces = max(1, depth // 256)
    dma = pltpu.SemaphoreType.DMA
    line_sems = [dma((lines, pieces))] * 4
    return pl.pallas_call(
        functools.partial(gather_kernel, lines, pieces),
        out_shape=(
            jax.ShapeDtypeStruct((tokens.shape[0], tokens.shape[1] * lax.axis_size("kv")), tokens.dtype),
            jax.ShapeDtypeStruct((depth * lax.axis_size("ctx"), width), weights.dtype),
        ),
        in_specs=[pl.BlockSpec(memory_space=pl.ANY)] * 2,
        out_specs=[pl.BlockSpec(memory_space=pl.ANY)] * 2,
        scratch_shapes=[dma((2,)), dma((3,)), dma((3,))] + line_sems
        + [dma((2 * lines - 1, pieces))] * 2,
        compiler_params=pltpu.CompilerParams(collective_id=0, has_side_effects=True),
    )(tokens, weights)


def shards(tokens, segment_ids, query_weight, key_weight, value_projection_matrix):
    rows = tokens.shape[0]
    packed = jnp.concatenate([key_weight, value_projection_matrix, query_weight], axis=1)
    whole, weights = gathered(tokens, packed)
    wide = key_weight.shape[1]
    key_value = jnp.dot(whole, weights[:, :2 * wide], preferred_element_type=jnp.float32).astype(jnp.bfloat16)
    key_rows, value_rows = key_value[:, :wide], key_value[:, wide:]
    query_rows = jnp.dot(whole, weights[:, 2 * wide:], preferred_element_type=jnp.float32).astype(jnp.bfloat16)
    prev_key, prev_value = shifted((key_rows, value_rows), "ctx", 1)
    kv_heads = key_weight.shape[1] // HEAD_DIMENSION
    query_group = query_weight.shape[1] // (HEAD_DIMENSION * kv_heads)
    query_matrix = query_rows.reshape(rows, kv_heads, query_group, HEAD_DIMENSION)
    nearby_keys = jnp.concatenate([prev_key, key_rows], axis=0).reshape(
        2 * rows, kv_heads, HEAD_DIMENSION
    )
    nearby_values = jnp.concatenate([prev_value, value_rows], axis=0).reshape(
        2 * rows, kv_heads, HEAD_DIMENSION
    )
    position = lax.axis_index("ctx")
    begin_offset = position * rows
    prev_start = jnp.maximum(begin_offset - rows, 0)
    seg_query = lax.dynamic_slice_in_dim(segment_ids, begin_offset, rows, 0)
    seg_prev = lax.dynamic_slice_in_dim(segment_ids, prev_start, rows, 0)
    seg_keys = jnp.concatenate([seg_prev, seg_query], axis=0)
    qpos = begin_offset + jnp.arange(rows, dtype=jnp.int32)
    kpos = begin_offset - rows + jnp.arange(2 * rows, dtype=jnp.int32)
    visible = (kpos[None, :] <= qpos[:, None]) & (kpos[None, :] > qpos[:, None] - rows)
    visible = visible & (kpos[None, :] >= 0) & (seg_keys[None, :] == seg_query[:, None])
    return attend_block(query_matrix, nearby_keys, nearby_values, visible)


def solution(mesh):
    placed = (P("ctx", "kv"), P(), P("ctx", "kv"), P("ctx", "kv"), P("ctx", "kv"))
    return jax.shard_map(
        shards, mesh=mesh, in_specs=placed, out_specs=P("ctx", "kv"), check_vma=False
    )
```

```python
import functools

import jax
import jax.numpy as jnp
from jax import lax
from jax.experimental import pallas as pl
from jax.experimental.pallas import tpu as pltpu
from jax.sharding import PartitionSpec as P

HEAD_DIMENSION = 128


def shifted(shard, axis, by):
    length = lax.axis_size(axis)
    pairs = [(i, i + by) for i in range(length) if 0 <= i + by < length]
    return lax.ppermute(shard, axis, pairs)


def attend_block(query_matrix, key_matrix, value_matrix, visible):
    head_size = query_matrix.shape[-1]
    scores = jnp.einsum(
        "thgd,shd->hgts", query_matrix, key_matrix, preferred_element_type=jnp.float32
    ) * head_size ** (-0.5)
    scores = jnp.where(visible[None, None], scores, -1e30)
    largest = jnp.max(scores, axis=-1, keepdims=True)
    expon = jnp.where(visible[None, None], jnp.exp(scores - largest), 0.0)
    total = jnp.sum(expon, axis=-1, keepdims=True)
    weights = expon.astype(jnp.bfloat16)
    summed = jnp.einsum("hgts,shd->hgtd", weights, value_matrix, preferred_element_type=jnp.float32)
    result = summed / total
    rows = query_matrix.shape[0]
    return jnp.transpose(result, (2, 0, 1, 3)).reshape(rows, -1).astype(jnp.bfloat16)


MESH = pl.DeviceIdType.MESH


def gather_kernel(lines, pieces, tok, wgt, mine, theirs, wgt_all, loc, ts, tr,
                  up_s, up_r, dn_s, dn_r, y_s, y_r):
    ctx, kv = lax.axis_index("ctx"), lax.axis_index("kv")
    z, y = ctx // 2, ctx % 2
    up, down, across = {"ctx": ctx + 2}, {"ctx": ctx - 2}, {"ctx": z * 2 + (1 - y)}
    other_core, other_chip = (kv // 2) * 2 + (1 - kv % 2), (1 - kv // 2) * 2 + kv % 2
    core, far = {"kv": other_core}, {"kv": other_chip}
    has_up, has_down = z < lines - 1, z > 0
    height, depth = tok.shape[1], wgt.shape[1]
    rows = depth // pieces

    barrier = pltpu.get_barrier_semaphore()
    for other in (across, core, far):
        pl.semaphore_signal(barrier, inc=1, device_id=other, device_id_type=MESH)

    @pl.when(has_up)
    def _():
        pl.semaphore_signal(barrier, inc=1, device_id=up, device_id_type=MESH)

    @pl.when(has_down)
    def _():
        pl.semaphore_signal(barrier, inc=1, device_id=down, device_id_type=MESH)

    pl.semaphore_wait(barrier, 3 + has_up.astype(jnp.int32) + has_down.astype(jnp.int32))

    def copy(src, dst, send, recv, other):
        return pltpu.make_async_remote_copy(
            src_ref=src, dst_ref=dst, send_sem=send, recv_sem=recv,
            device_id=other, device_id_type=MESH)

    def place(line, side, p):
        start = pl.multiple_of((line * 2 + side) * depth + p * rows, rows)
        return wgt_all.at[pl.ds(start, rows), :]

    def own(half, p):
        return wgt.at[half, pl.ds(p * rows, rows), :]

    def block(off, s, p):
        return own(y, p) if (off, s) == (0, 0) else place(z + off, y if s == 0 else 1 - y, p)

    def up_copy(d, s, p):
        dst = place(z - d, y if s == 0 else 1 - y, p)
        return copy(block(-d, s, p), dst, up_s.at[d, s, p], up_r.at[d, s, p], up)

    def down_copy(d, s, p):
        dst = place(z + d, y if s == 0 else 1 - y, p)
        return copy(block(d, s, p), dst, dn_s.at[d, s, p], dn_r.at[d, s, p], down)

    def y_copy(p):
        return copy(own(1 - y, p), place(z, y, p), y_s.at[p], y_r.at[p], across)

    def columns(ref, k):
        return ref.at[:, pl.ds(pl.multiple_of(k * height, height), height)]

    def both_ways(d, s, p):
        pl.when(has_up)(lambda: up_copy(d, s, p).start())
        pl.when(has_down)(lambda: down_copy(d, s, p).start())

    own_far = copy(tok, columns(mine, kv), ts.at[0], tr.at[0], far)
    own_core = copy(tok, columns(mine, kv), ts.at[1], tr.at[1], core)
    own_across = copy(tok, columns(theirs, kv), ts.at[2], tr.at[2], across)
    mine_core = copy(columns(mine, other_chip), columns(mine, other_chip), ts.at[3], tr.at[3], core)
    their_far = copy(columns(theirs, kv), columns(theirs, kv), ts.at[4], tr.at[4], far)
    their_core = copy(columns(theirs, kv), columns(theirs, kv), ts.at[5], tr.at[5], core)
    last_core = copy(columns(theirs, other_chip), columns(theirs, other_chip), ts.at[6], tr.at[6], core)

    for p in range(pieces):
        y_copy(p).start()
        both_ways(0, 0, p)
    own_far.start()
    own_across.start()
    own_core.start()
    local = [pltpu.make_async_copy(tok, columns(mine, kv), loc.at[0]),
             pltpu.make_async_copy(
                 wgt.at[y], wgt_all.at[pl.ds(pl.multiple_of(ctx * depth, depth), depth), :], loc.at[1])]
    for c in local:
        c.start()
    for p in range(pieces):
        y_copy(p).wait_recv()
        both_ways(0, 1, p)

    def relay_mine():
        own_far.wait_recv()
        mine_core.start()

    def relay_theirs():
        own_across.wait_recv()
        their_far.start()
        their_core.start()

    def relay_last():
        their_far.wait_recv()
        last_core.start()

    relays = {(1, 1): relay_mine, (2, 0): relay_theirs, (3, 0): relay_last}
    for d in range(1, lines):
        for s in range(2):
            for p in range(pieces):
                @pl.when(z >= d)
                def _(d=d, s=s, p=p):
                    up_copy(d - 1, s, p).wait_recv()
                    if d < lines - 1:
                        pl.when(has_up)(lambda: up_copy(d, s, p).start())

                @pl.when(z + d < lines)
                def _(d=d, s=s, p=p):
                    down_copy(d - 1, s, p).wait_recv()
                    if d < lines - 1:
                        pl.when(has_down)(lambda: down_copy(d, s, p).start())
            if (d, s) in relays:
                relays.pop((d, s))()
    for key in sorted(relays):
        relays[key]()

    for c in (own_core, mine_core, their_core, last_core):
        c.wait_recv()
    for c in (own_far, own_core, own_across, mine_core, their_far, their_core, last_core):
        c.wait_send()
    for c in local:
        c.wait()
    for p in range(pieces):
        y_copy(p).wait_send()
        for s in range(2):
            for d in range(lines - 1):
                pl.when(has_up & (z >= d))(lambda d=d, s=s, p=p: up_copy(d, s, p).wait_send())
                pl.when(has_down & (z + d < lines))(
                    lambda d=d, s=s, p=p: down_copy(d, s, p).wait_send())


def gathered(tokens, weights):
    lines = lax.axis_size("ctx") // 2
    _, depth, width = weights.shape
    pieces = max(1, depth // 256)
    dma = pltpu.SemaphoreType.DMA
    line_sems = [dma((lines, 2, pieces))] * 4
    all_features = jax.ShapeDtypeStruct(
        (tokens.shape[0], tokens.shape[1] * lax.axis_size("kv")), tokens.dtype)
    return pl.pallas_call(
        functools.partial(gather_kernel, lines, pieces),
        out_shape=(
            all_features,
            all_features,
            jax.ShapeDtypeStruct((depth * lax.axis_size("ctx"), width), weights.dtype),
        ),
        in_specs=[pl.BlockSpec(memory_space=pl.ANY)] * 2,
        out_specs=[pl.BlockSpec(memory_space=pl.ANY)] * 3,
        scratch_shapes=[dma((2,)), dma((7,)), dma((7,))] + line_sems + [dma((pieces,))] * 2,
        compiler_params=pltpu.CompilerParams(collective_id=0, has_side_effects=True),
    )(tokens, weights)


def shards(tokens, segment_ids, query_weight, key_weight, value_projection_matrix):
    rows = tokens.shape[0]
    wide, half = key_weight.shape[1], query_weight.shape[1] // 2
    packed = jnp.stack([
        jnp.concatenate([key_weight, query_weight[:, :half]], axis=1),
        jnp.concatenate([value_projection_matrix, query_weight[:, half:]], axis=1),
    ])
    mine, theirs, weights = gathered(tokens, packed)

    def project(whole):
        return jnp.dot(whole, weights, preferred_element_type=jnp.float32).astype(jnp.bfloat16)

    pairs = [(i, i ^ 1) for i in range(lax.axis_size("ctx"))]
    received = lax.ppermute(project(theirs), "ctx", pairs)
    kept = project(mine)
    first_side = lax.axis_index("ctx") % 2 == 0
    low = jnp.where(first_side, kept, received)
    high = jnp.where(first_side, received, kept)
    key_rows, value_rows = low[:, :wide], high[:, :wide]
    query_rows = jnp.concatenate([low[:, wide:], high[:, wide:]], axis=1)
    prev_key, prev_value = shifted((key_rows, value_rows), "ctx", 1)
    kv_heads = key_weight.shape[1] // HEAD_DIMENSION
    query_group = query_weight.shape[1] // (HEAD_DIMENSION * kv_heads)
    query_matrix = query_rows.reshape(rows, kv_heads, query_group, HEAD_DIMENSION)
    nearby_keys = jnp.concatenate([prev_key, key_rows], axis=0).reshape(
        2 * rows, kv_heads, HEAD_DIMENSION
    )
    nearby_values = jnp.concatenate([prev_value, value_rows], axis=0).reshape(
        2 * rows, kv_heads, HEAD_DIMENSION
    )
    position = lax.axis_index("ctx")
    begin_offset = position * rows
    prev_start = jnp.maximum(begin_offset - rows, 0)
    seg_query = lax.dynamic_slice_in_dim(segment_ids, begin_offset, rows, 0)
    seg_prev = lax.dynamic_slice_in_dim(segment_ids, prev_start, rows, 0)
    seg_keys = jnp.concatenate([seg_prev, seg_query], axis=0)
    qpos = begin_offset + jnp.arange(rows, dtype=jnp.int32)
    kpos = begin_offset - rows + jnp.arange(2 * rows, dtype=jnp.int32)
    visible = (kpos[None, :] <= qpos[:, None]) & (kpos[None, :] > qpos[:, None] - rows)
    visible = visible & (kpos[None, :] >= 0) & (seg_keys[None, :] == seg_query[:, None])
    return attend_block(query_matrix, nearby_keys, nearby_values, visible)


def solution(mesh):
    placed = (P("ctx", "kv"), P(), P("ctx", "kv"), P("ctx", "kv"), P("ctx", "kv"))
    return jax.shard_map(
        shards, mesh=mesh, in_specs=placed, out_specs=P("ctx", "kv"), check_vma=False
    )
```

```python
import functools

import jax
import jax.numpy as jnp
from jax import lax
from jax.experimental import pallas as pl
from jax.experimental.pallas import tpu as pltpu
from jax.sharding import PartitionSpec as P

HEAD_DIMENSION = 128


def shifted(shard, axis, by):
    length = lax.axis_size(axis)
    pairs = [(i, i + by) for i in range(length) if 0 <= i + by < length]
    return lax.ppermute(shard, axis, pairs)


def attend_block(query_matrix, key_matrix, value_matrix, visible):
    head_size = query_matrix.shape[-1]
    scores = jnp.einsum(
        "thgd,shd->hgts", query_matrix, key_matrix, preferred_element_type=jnp.float32
    ) * head_size ** (-0.5)
    scores = jnp.where(visible[None, None], scores, -1e30)
    largest = jnp.max(scores, axis=-1, keepdims=True)
    expon = jnp.where(visible[None, None], jnp.exp(scores - largest), 0.0)
    total = jnp.sum(expon, axis=-1, keepdims=True)
    weights = expon.astype(jnp.bfloat16)
    summed = jnp.einsum("hgts,shd->hgtd", weights, value_matrix, preferred_element_type=jnp.float32)
    result = summed / total
    rows = query_matrix.shape[0]
    return jnp.transpose(result, (2, 0, 1, 3)).reshape(rows, -1).astype(jnp.bfloat16)


MESH = pl.DeviceIdType.MESH


def gather_kernel(lines, pieces, tok, wgt, mine, theirs, wgt_all, loc, ts, tr,
                  up_s, up_r, dn_s, dn_r, y_s, y_r):
    ctx, kv = lax.axis_index("ctx"), lax.axis_index("kv")
    z, y = ctx // 2, ctx % 2
    up, down, across = {"ctx": ctx + 2}, {"ctx": ctx - 2}, {"ctx": z * 2 + (1 - y)}
    other_core, other_chip = (kv // 2) * 2 + (1 - kv % 2), (1 - kv // 2) * 2 + kv % 2
    core, far = {"kv": other_core}, {"kv": other_chip}
    has_up, has_down = z < lines - 1, z > 0
    height, depth = tok.shape[1], wgt.shape[1]
    rows = depth // pieces

    barrier = pltpu.get_barrier_semaphore()
    for other in (across, core, far):
        pl.semaphore_signal(barrier, inc=1, device_id=other, device_id_type=MESH)

    @pl.when(has_up)
    def _():
        pl.semaphore_signal(barrier, inc=1, device_id=up, device_id_type=MESH)

    @pl.when(has_down)
    def _():
        pl.semaphore_signal(barrier, inc=1, device_id=down, device_id_type=MESH)

    pl.semaphore_wait(barrier, 3 + has_up.astype(jnp.int32) + has_down.astype(jnp.int32))

    def copy(src, dst, send, recv, other):
        return pltpu.make_async_remote_copy(
            src_ref=src, dst_ref=dst, send_sem=send, recv_sem=recv,
            device_id=other, device_id_type=MESH)

    def place(line, side, p):
        start = pl.multiple_of((line * 2 + side) * depth + p * rows, rows)
        return wgt_all.at[pl.ds(start, rows), :]

    def own(half, p):
        return wgt.at[half, pl.ds(p * rows, rows), :]

    def block(off, s, p):
        return own(y, p) if (off, s) == (0, 0) else place(z + off, y if s == 0 else 1 - y, p)

    def up_copy(d, s, p):
        dst = place(z - d, y if s == 0 else 1 - y, p)
        return copy(block(-d, s, p), dst, up_s.at[d, s, p], up_r.at[d, s, p], up)

    def down_copy(d, s, p):
        dst = place(z + d, y if s == 0 else 1 - y, p)
        return copy(block(d, s, p), dst, dn_s.at[d, s, p], dn_r.at[d, s, p], down)

    def y_copy(p):
        return copy(own(1 - y, p), place(z, y, p), y_s.at[p], y_r.at[p], across)

    def columns(ref, k):
        return ref.at[:, pl.ds(pl.multiple_of(k * height, height), height)]

    def both_ways(d, s, p):
        pl.when(has_up)(lambda: up_copy(d, s, p).start())
        pl.when(has_down)(lambda: down_copy(d, s, p).start())

    own_far = copy(tok, columns(mine, kv), ts.at[0], tr.at[0], far)
    own_core = copy(tok, columns(mine, kv), ts.at[1], tr.at[1], core)
    own_across = copy(tok, columns(theirs, kv), ts.at[2], tr.at[2], across)
    mine_core = copy(columns(mine, other_chip), columns(mine, other_chip), ts.at[3], tr.at[3], core)
    their_far = copy(columns(theirs, kv), columns(theirs, kv), ts.at[4], tr.at[4], far)
    their_core = copy(columns(theirs, kv), columns(theirs, kv), ts.at[5], tr.at[5], core)
    last_core = copy(columns(theirs, other_chip), columns(theirs, other_chip), ts.at[6], tr.at[6], core)

    for p in range(pieces):
        y_copy(p).start()
        both_ways(0, 0, p)
    own_far.start()
    own_across.start()
    own_core.start()
    local = [pltpu.make_async_copy(tok, columns(mine, kv), loc.at[0]),
             pltpu.make_async_copy(
                 wgt.at[y], wgt_all.at[pl.ds(pl.multiple_of(ctx * depth, depth), depth), :], loc.at[1])]
    for c in local:
        c.start()
    for p in range(pieces):
        y_copy(p).wait_recv()
        both_ways(0, 1, p)

    def relay_mine():
        own_far.wait_recv()
        mine_core.start()

    def relay_theirs():
        own_across.wait_recv()
        their_far.start()
        their_core.start()

    def relay_last():
        their_far.wait_recv()
        last_core.start()

    relays = {(1, 1): relay_mine, (2, 0): relay_theirs, (3, 0): relay_last}
    for d in range(1, lines):
        for s in range(2):
            for p in range(pieces):
                @pl.when(z >= d)
                def _(d=d, s=s, p=p):
                    up_copy(d - 1, s, p).wait_recv()
                    if d < lines - 1:
                        pl.when(has_up)(lambda: up_copy(d, s, p).start())

                @pl.when(z + d < lines)
                def _(d=d, s=s, p=p):
                    down_copy(d - 1, s, p).wait_recv()
                    if d < lines - 1:
                        pl.when(has_down)(lambda: down_copy(d, s, p).start())
            if (d, s) in relays:
                relays.pop((d, s))()
    for key in sorted(relays):
        relays[key]()

    for c in (own_core, mine_core, their_core, last_core):
        c.wait_recv()
    for c in (own_far, own_core, own_across, mine_core, their_far, their_core, last_core):
        c.wait_send()
    for c in local:
        c.wait()
    for p in range(pieces):
        y_copy(p).wait_send()
        for s in range(2):
            for d in range(lines - 1):
                pl.when(has_up & (z >= d))(lambda d=d, s=s, p=p: up_copy(d, s, p).wait_send())
                pl.when(has_down & (z + d < lines))(
                    lambda d=d, s=s, p=p: down_copy(d, s, p).wait_send())


def gathered(tokens, weights):
    lines = lax.axis_size("ctx") // 2
    _, depth, width = weights.shape
    pieces = max(1, depth // 256)
    dma = pltpu.SemaphoreType.DMA
    line_sems = [dma((lines, 2, pieces))] * 4
    all_features = jax.ShapeDtypeStruct(
        (tokens.shape[0], tokens.shape[1] * lax.axis_size("kv")), tokens.dtype)
    return pl.pallas_call(
        functools.partial(gather_kernel, lines, pieces),
        out_shape=(
            all_features,
            all_features,
            jax.ShapeDtypeStruct((depth * lax.axis_size("ctx"), width), weights.dtype),
        ),
        in_specs=[pl.BlockSpec(memory_space=pl.ANY)] * 2,
        out_specs=[pl.BlockSpec(memory_space=pl.ANY)] * 3,
        scratch_shapes=[dma((2,)), dma((7,)), dma((7,))] + line_sems + [dma((pieces,))] * 2,
        compiler_params=pltpu.CompilerParams(collective_id=0, has_side_effects=True),
    )(tokens, weights)


def shards(tokens, segment_ids, query_weight, key_weight, value_projection_matrix):
    rows = tokens.shape[0]
    wide, half = key_weight.shape[1], query_weight.shape[1] // 2
    packed = jnp.stack([
        jnp.concatenate([key_weight, query_weight[:, :half]], axis=1),
        jnp.concatenate([value_projection_matrix, query_weight[:, half:]], axis=1),
    ])
    mine, theirs, weights = gathered(tokens, packed)

    def project(whole):
        return jnp.dot(whole, weights, preferred_element_type=jnp.float32).astype(jnp.bfloat16)

    pairs = [(i, i ^ 1) for i in range(lax.axis_size("ctx"))]
    received = lax.ppermute(project(theirs), "ctx", pairs)
    kept, received = lax.optimization_barrier((project(mine), received))
    first_side = lax.axis_index("ctx") % 2 == 0
    low = jnp.where(first_side, kept, received)
    high = jnp.where(first_side, received, kept)
    key_rows, value_rows = low[:, :wide], high[:, :wide]
    query_rows = jnp.concatenate([low[:, wide:], high[:, wide:]], axis=1)
    prev_key, prev_value = shifted((key_rows, value_rows), "ctx", 1)
    kv_heads = key_weight.shape[1] // HEAD_DIMENSION
    query_group = query_weight.shape[1] // (HEAD_DIMENSION * kv_heads)
    query_matrix = query_rows.reshape(rows, kv_heads, query_group, HEAD_DIMENSION)
    nearby_keys = jnp.concatenate([prev_key, key_rows], axis=0).reshape(
        2 * rows, kv_heads, HEAD_DIMENSION
    )
    nearby_values = jnp.concatenate([prev_value, value_rows], axis=0).reshape(
        2 * rows, kv_heads, HEAD_DIMENSION
    )
    position = lax.axis_index("ctx")
    begin_offset = position * rows
    prev_start = jnp.maximum(begin_offset - rows, 0)
    seg_query = lax.dynamic_slice_in_dim(segment_ids, begin_offset, rows, 0)
    seg_prev = lax.dynamic_slice_in_dim(segment_ids, prev_start, rows, 0)
    seg_keys = jnp.concatenate([seg_prev, seg_query], axis=0)
    qpos = begin_offset + jnp.arange(rows, dtype=jnp.int32)
    kpos = begin_offset - rows + jnp.arange(2 * rows, dtype=jnp.int32)
    visible = (kpos[None, :] <= qpos[:, None]) & (kpos[None, :] > qpos[:, None] - rows)
    visible = visible & (kpos[None, :] >= 0) & (seg_keys[None, :] == seg_query[:, None])
    return attend_block(query_matrix, nearby_keys, nearby_values, visible)


def solution(mesh):
    placed = (P("ctx", "kv"), P(), P("ctx", "kv"), P("ctx", "kv"), P("ctx", "kv"))
    return jax.shard_map(
        shards, mesh=mesh, in_specs=placed, out_specs=P("ctx", "kv"), check_vma=False
    )
```

```python
import functools

import jax
import jax.numpy as jnp
from jax import lax
from jax.experimental import pallas as pl
from jax.experimental.pallas import tpu as pltpu
from jax.sharding import PartitionSpec as P

HEAD_DIMENSION = 128


def shifted(shard, axis, by):
    length = lax.axis_size(axis)
    pairs = [(i, i + by) for i in range(length) if 0 <= i + by < length]
    return lax.ppermute(shard, axis, pairs)


def attend_block(query_matrix, key_matrix, value_matrix, visible):
    head_size = query_matrix.shape[-1]
    scores = jnp.einsum(
        "thgd,shd->hgts", query_matrix, key_matrix, preferred_element_type=jnp.float32
    ) * head_size ** (-0.5)
    scores = jnp.where(visible[None, None], scores, -1e30)
    largest = jnp.max(scores, axis=-1, keepdims=True)
    expon = jnp.where(visible[None, None], jnp.exp(scores - largest), 0.0)
    total = jnp.sum(expon, axis=-1, keepdims=True)
    weights = expon.astype(jnp.bfloat16)
    summed = jnp.einsum("hgts,shd->hgtd", weights, value_matrix, preferred_element_type=jnp.float32)
    result = summed / total
    rows = query_matrix.shape[0]
    return jnp.transpose(result, (2, 0, 1, 3)).reshape(rows, -1).astype(jnp.bfloat16)


MESH = pl.DeviceIdType.MESH


def gather_kernel(lines, pieces, tok, wgt, zeros, mine, theirs, wgt_all, ext_mine, ext_theirs, loc, ts, tr,
                  up_s, up_r, dn_s, dn_r, y_s, y_r):
    ctx, kv = lax.axis_index("ctx"), lax.axis_index("kv")
    z, y = ctx // 2, ctx % 2
    up, down, across = {"ctx": ctx + 2}, {"ctx": ctx - 2}, {"ctx": z * 2 + (1 - y)}
    other_core, other_chip = (kv // 2) * 2 + (1 - kv % 2), (1 - kv // 2) * 2 + kv % 2
    core, far = {"kv": other_core}, {"kv": other_chip}
    has_up, has_down = z < lines - 1, z > 0
    height, depth = tok.shape[1], wgt.shape[1]
    rows = depth // pieces

    barrier = pltpu.get_barrier_semaphore()
    for other in (across, core, far):
        pl.semaphore_signal(barrier, inc=1, device_id=other, device_id_type=MESH)

    @pl.when(has_up)
    def _():
        pl.semaphore_signal(barrier, inc=1, device_id=up, device_id_type=MESH)

    @pl.when(has_down)
    def _():
        pl.semaphore_signal(barrier, inc=1, device_id=down, device_id_type=MESH)

    pl.semaphore_wait(barrier, 3 + has_up.astype(jnp.int32) + has_down.astype(jnp.int32))

    def copy(src, dst, send, recv, other):
        return pltpu.make_async_remote_copy(
            src_ref=src, dst_ref=dst, send_sem=send, recv_sem=recv,
            device_id=other, device_id_type=MESH)

    def place(line, side, p):
        start = pl.multiple_of((line * 2 + side) * depth + p * rows, rows)
        return wgt_all.at[pl.ds(start, rows), :]

    def own(half, p):
        return wgt.at[half, pl.ds(p * rows, rows), :]

    def block(off, s, p):
        return own(y, p) if (off, s) == (0, 0) else place(z + off, y if s == 0 else 1 - y, p)

    def up_copy(d, s, p):
        dst = place(z - d, y if s == 0 else 1 - y, p)
        return copy(block(-d, s, p), dst, up_s.at[d, s, p], up_r.at[d, s, p], up)

    def down_copy(d, s, p):
        dst = place(z + d, y if s == 0 else 1 - y, p)
        return copy(block(d, s, p), dst, dn_s.at[d, s, p], dn_r.at[d, s, p], down)

    def y_copy(p):
        return copy(own(1 - y, p), place(z, y, p), y_s.at[p], y_r.at[p], across)

    def columns(ref, k):
        return ref.at[:, pl.ds(pl.multiple_of(k * height, height), height)]

    def both_ways(d, s, p):
        pl.when(has_up)(lambda: up_copy(d, s, p).start())
        pl.when(has_down)(lambda: down_copy(d, s, p).start())

    own_far = copy(tok, columns(mine, kv), ts.at[0], tr.at[0], far)
    own_core = copy(tok, columns(mine, kv), ts.at[1], tr.at[1], core)
    own_across = copy(tok, columns(theirs, kv), ts.at[2], tr.at[2], across)
    mine_core = copy(columns(mine, other_chip), columns(mine, other_chip), ts.at[3], tr.at[3], core)
    their_far = copy(columns(theirs, kv), columns(theirs, kv), ts.at[4], tr.at[4], far)
    their_core = copy(columns(theirs, kv), columns(theirs, kv), ts.at[5], tr.at[5], core)
    last_core = copy(columns(theirs, other_chip), columns(theirs, other_chip), ts.at[6], tr.at[6], core)

    for p in range(pieces):
        y_copy(p).start()
        both_ways(0, 0, p)
    own_far.start()
    own_across.start()
    own_core.start()
    edge, inner = (z == 0) | (z == lines - 1), (z == 1) | (z == lines - 2)
    core_index, strip = kv % 2, tok.shape[0] // 2
    opposite = (lines - 1) * (1 - jnp.minimum(z, 1))
    strip_rows = pl.ds(pl.multiple_of(core_index * strip, strip), strip)
    needed = pl.ds(pl.multiple_of(opposite * 2 * depth, 2 * depth), 2 * depth)

    def edge_copy(other):
        return copy(mine.at[strip_rows, needed], ext_mine.at[strip_rows, :], ts.at[7], tr.at[7], other)

    ext_across = copy(ext_mine.at[strip_rows, :], ext_theirs.at[strip_rows, :], ts.at[8], tr.at[8], across)
    ext_core = copy(ext_mine.at[strip_rows, :], ext_mine.at[strip_rows, :], ts.at[9], tr.at[9], core)
    ext_last = copy(ext_theirs.at[strip_rows, :], ext_theirs.at[strip_rows, :], ts.at[10], tr.at[10], core)
    fill = pltpu.make_async_copy(zeros, wgt_all.at[needed, :], loc.at[2])
    pl.when(edge)(lambda: fill.start())
    local = [pltpu.make_async_copy(tok, columns(mine, kv), loc.at[0]),
             pltpu.make_async_copy(
                 wgt.at[y], wgt_all.at[pl.ds(pl.multiple_of(ctx * depth, depth), depth), :], loc.at[1])]
    for c in local:
        c.start()
    for p in range(pieces):
        y_copy(p).wait_recv()
        both_ways(0, 1, p)

    def relay_mine():
        own_far.wait_recv()
        mine_core.start()
        own_core.wait_recv()
        mine_core.wait_recv()
        local[0].wait()
        pl.when(z == 0)(lambda: edge_copy(up).start())
        pl.when(z == lines - 1)(lambda: edge_copy(down).start())

    def relay_theirs():
        own_across.wait_recv()
        their_far.start()
        their_core.start()

    def relay_ext():
        @pl.when(inner)
        def _():
            edge_copy(core).wait_recv()
            ext_across.start()
            ext_core.start()

    relays = {(1, 0): relay_mine, (1, 1): relay_theirs, (2, 0): relay_ext}
    for d in range(1, lines - 1):
        for s in range(2):
            for p in range(pieces):
                @pl.when(z >= d)
                def _(d=d, s=s, p=p):
                    up_copy(d - 1, s, p).wait_recv()
                    if d < lines - 2:
                        pl.when(has_up)(lambda: up_copy(d, s, p).start())

                @pl.when(z + d < lines)
                def _(d=d, s=s, p=p):
                    down_copy(d - 1, s, p).wait_recv()
                    if d < lines - 2:
                        pl.when(has_down)(lambda: down_copy(d, s, p).start())
            if (d, s) in relays:
                relays.pop((d, s))()
    for key in sorted(relays):
        relays[key]()

    their_far.wait_recv()
    last_core.start()

    @pl.when(inner)
    def _():
        ext_across.wait_recv()
        ext_last.start()
        ext_core.wait_recv()
        ext_last.wait_recv()
        for c in (ext_across, ext_core, ext_last):
            c.wait_send()

    @pl.when(edge)
    def _():
        edge_copy(core).wait_send()
        fill.wait()

    for c in (their_core, last_core):
        c.wait_recv()
    for c in (own_far, own_core, own_across, mine_core, their_far, their_core, last_core):
        c.wait_send()
    local[1].wait()
    for p in range(pieces):
        y_copy(p).wait_send()
        for s in range(2):
            for d in range(lines - 2):
                pl.when(has_up & (z >= d))(lambda d=d, s=s, p=p: up_copy(d, s, p).wait_send())
                pl.when(has_down & (z + d < lines))(
                    lambda d=d, s=s, p=p: down_copy(d, s, p).wait_send())


def gathered(tokens, weights):
    lines = lax.axis_size("ctx") // 2
    _, depth, width = weights.shape
    pieces = max(1, depth // 256)
    dma = pltpu.SemaphoreType.DMA
    line_sems = [dma((lines, 2, pieces))] * 4
    all_features = jax.ShapeDtypeStruct(
        (tokens.shape[0], tokens.shape[1] * lax.axis_size("kv")), tokens.dtype)
    strip = jax.ShapeDtypeStruct((tokens.shape[0], 2 * depth), tokens.dtype)
    return pl.pallas_call(
        functools.partial(gather_kernel, lines, pieces),
        out_shape=(
            all_features,
            all_features,
            jax.ShapeDtypeStruct((depth * lax.axis_size("ctx"), width), weights.dtype),
            strip,
            strip,
        ),
        in_specs=[pl.BlockSpec(memory_space=pl.ANY)] * 3,
        out_specs=[pl.BlockSpec(memory_space=pl.ANY)] * 5,
        scratch_shapes=[dma((3,)), dma((11,)), dma((11,))] + line_sems + [dma((pieces,))] * 2,
        compiler_params=pltpu.CompilerParams(collective_id=0, has_side_effects=True),
    )(tokens, weights, jnp.zeros((2 * depth, width), weights.dtype))


def shards(tokens, segment_ids, query_weight, key_weight, value_projection_matrix):
    rows = tokens.shape[0]
    wide, half = key_weight.shape[1], query_weight.shape[1] // 2
    packed = jnp.stack([
        jnp.concatenate([key_weight, query_weight[:, :half]], axis=1),
        jnp.concatenate([value_projection_matrix, query_weight[:, half:]], axis=1),
    ])
    mine, theirs, weights, ext_mine, ext_theirs = gathered(tokens, packed)
    length, block = lax.axis_size("ctx"), 2 * query_weight.shape[0]
    pairs = [(i, i ^ 1) for i in range(length)]
    inward = [(2, 0), (3, 1), (length - 4, length - 2), (length - 3, length - 1)]
    begin = jnp.where(lax.axis_index("ctx") // 2 == 1, weights.shape[0] - block, 0)
    opposite = lax.dynamic_slice_in_dim(weights, begin, block, 0)

    def project(whole, matrix):
        return jnp.dot(whole, matrix, preferred_element_type=jnp.float32)

    def help_end(ext):
        return lax.ppermute(project(ext, opposite).astype(jnp.bfloat16), "ctx", inward)

    def whole_sum(whole, helped):
        own, helped = lax.optimization_barrier((project(whole, weights), helped))
        return (own + helped.astype(jnp.float32)).astype(jnp.bfloat16)

    helped_theirs, helped_mine = help_end(ext_theirs), help_end(ext_mine)
    received = lax.ppermute(whole_sum(theirs, helped_theirs), "ctx", pairs)
    kept = whole_sum(mine, helped_mine)
    first_side = lax.axis_index("ctx") % 2 == 0
    low = jnp.where(first_side, kept, received)
    high = jnp.where(first_side, received, kept)
    key_rows, value_rows = low[:, :wide], high[:, :wide]
    query_rows = jnp.concatenate([low[:, wide:], high[:, wide:]], axis=1)
    prev_key, prev_value = shifted((key_rows, value_rows), "ctx", 1)
    kv_heads = key_weight.shape[1] // HEAD_DIMENSION
    query_group = query_weight.shape[1] // (HEAD_DIMENSION * kv_heads)
    query_matrix = query_rows.reshape(rows, kv_heads, query_group, HEAD_DIMENSION)
    nearby_keys = jnp.concatenate([prev_key, key_rows], axis=0).reshape(
        2 * rows, kv_heads, HEAD_DIMENSION
    )
    nearby_values = jnp.concatenate([prev_value, value_rows], axis=0).reshape(
        2 * rows, kv_heads, HEAD_DIMENSION
    )
    position = lax.axis_index("ctx")
    begin_offset = position * rows
    prev_start = jnp.maximum(begin_offset - rows, 0)
    seg_query = lax.dynamic_slice_in_dim(segment_ids, begin_offset, rows, 0)
    seg_prev = lax.dynamic_slice_in_dim(segment_ids, prev_start, rows, 0)
    seg_keys = jnp.concatenate([seg_prev, seg_query], axis=0)
    qpos = begin_offset + jnp.arange(rows, dtype=jnp.int32)
    kpos = begin_offset - rows + jnp.arange(2 * rows, dtype=jnp.int32)
    visible = (kpos[None, :] <= qpos[:, None]) & (kpos[None, :] > qpos[:, None] - rows)
    visible = visible & (kpos[None, :] >= 0) & (seg_keys[None, :] == seg_query[:, None])
    return attend_block(query_matrix, nearby_keys, nearby_values, visible)


def solution(mesh):
    placed = (P("ctx", "kv"), P(), P("ctx", "kv"), P("ctx", "kv"), P("ctx", "kv"))
    return jax.shard_map(
        shards, mesh=mesh, in_specs=placed, out_specs=P("ctx", "kv"), check_vma=False
    )
```

```python
import functools

import jax
import jax.numpy as jnp
from jax import lax
from jax.experimental import pallas as pl
from jax.experimental.pallas import tpu as pltpu
from jax.sharding import PartitionSpec as P

HEAD_DIMENSION = 128


def shifted(shard, axis, by):
    length = lax.axis_size(axis)
    pairs = [(i, i + by) for i in range(length) if 0 <= i + by < length]
    return lax.ppermute(shard, axis, pairs)


def attend_block(query_matrix, key_matrix, value_matrix, visible):
    head_size = query_matrix.shape[-1]
    scores = jnp.einsum(
        "thgd,shd->hgts", query_matrix, key_matrix, preferred_element_type=jnp.float32
    ) * head_size ** (-0.5)
    scores = jnp.where(visible[None, None], scores, -1e30)
    largest = jnp.max(scores, axis=-1, keepdims=True)
    expon = jnp.where(visible[None, None], jnp.exp(scores - largest), 0.0)
    total = jnp.sum(expon, axis=-1, keepdims=True)
    weights = expon.astype(jnp.bfloat16)
    summed = jnp.einsum("hgts,shd->hgtd", weights, value_matrix, preferred_element_type=jnp.float32)
    result = summed / total
    rows = query_matrix.shape[0]
    return jnp.transpose(result, (2, 0, 1, 3)).reshape(rows, -1).astype(jnp.bfloat16)


MESH = pl.DeviceIdType.MESH


def gather_kernel(lines, pieces, tok, wgt, zeros, mine, theirs, wgt_all, ext_mine, ext_theirs, loc, ts, tr,
                  up_s, up_r, dn_s, dn_r, y_s, y_r):
    ctx, kv = lax.axis_index("ctx"), lax.axis_index("kv")
    z, y = ctx // 2, ctx % 2
    up, down, across = {"ctx": ctx + 2}, {"ctx": ctx - 2}, {"ctx": z * 2 + (1 - y)}
    other_core, other_chip = (kv // 2) * 2 + (1 - kv % 2), (1 - kv // 2) * 2 + kv % 2
    core, far = {"kv": other_core}, {"kv": other_chip}
    has_up, has_down = z < lines - 1, z > 0
    height, depth = tok.shape[1], wgt.shape[1]
    rows = depth // pieces

    barrier = pltpu.get_barrier_semaphore()
    for other in (across, core, far):
        pl.semaphore_signal(barrier, inc=1, device_id=other, device_id_type=MESH)

    @pl.when(has_up)
    def _():
        pl.semaphore_signal(barrier, inc=1, device_id=up, device_id_type=MESH)

    @pl.when(has_down)
    def _():
        pl.semaphore_signal(barrier, inc=1, device_id=down, device_id_type=MESH)

    pl.semaphore_wait(barrier, 3 + has_up.astype(jnp.int32) + has_down.astype(jnp.int32))

    def copy(src, dst, send, recv, other):
        return pltpu.make_async_remote_copy(
            src_ref=src, dst_ref=dst, send_sem=send, recv_sem=recv,
            device_id=other, device_id_type=MESH)

    def place(line, side, p):
        start = pl.multiple_of((line * 2 + side) * depth + p * rows, rows)
        return wgt_all.at[pl.ds(start, rows), :]

    def own(half, p):
        return wgt.at[half, pl.ds(p * rows, rows), :]

    def block(off, s, p):
        return own(y, p) if (off, s) == (0, 0) else place(z + off, y if s == 0 else 1 - y, p)

    def up_copy(d, s, p):
        dst = place(z - d, y if s == 0 else 1 - y, p)
        return copy(block(-d, s, p), dst, up_s.at[d, s, p], up_r.at[d, s, p], up)

    def down_copy(d, s, p):
        dst = place(z + d, y if s == 0 else 1 - y, p)
        return copy(block(d, s, p), dst, dn_s.at[d, s, p], dn_r.at[d, s, p], down)

    def y_copy(p):
        return copy(own(1 - y, p), place(z, y, p), y_s.at[p], y_r.at[p], across)

    def columns(ref, k):
        return ref.at[:, pl.ds(pl.multiple_of(k * height, height), height)]

    def both_ways(d, s, p):
        pl.when(has_up)(lambda: up_copy(d, s, p).start())
        pl.when(has_down)(lambda: down_copy(d, s, p).start())

    own_far = copy(tok, columns(mine, kv), ts.at[0], tr.at[0], far)
    own_core = copy(tok, columns(mine, kv), ts.at[1], tr.at[1], core)
    own_across = copy(tok, columns(theirs, kv), ts.at[2], tr.at[2], across)
    mine_core = copy(columns(mine, other_chip), columns(mine, other_chip), ts.at[3], tr.at[3], core)
    their_far = copy(columns(theirs, kv), columns(theirs, kv), ts.at[4], tr.at[4], far)
    their_core = copy(columns(theirs, kv), columns(theirs, kv), ts.at[5], tr.at[5], core)
    last_core = copy(columns(theirs, other_chip), columns(theirs, other_chip), ts.at[6], tr.at[6], core)

    own_across.start()
    own_far.start()
    own_core.start()
    for p in range(pieces):
        both_ways(0, 0, p)
    for p in range(pieces):
        y_copy(p).start()
    edge, inner = (z == 0) | (z == lines - 1), (z == 1) | (z == lines - 2)
    core_index, strip = kv % 2, tok.shape[0] // 2
    opposite = (lines - 1) * (1 - jnp.minimum(z, 1))
    strip_rows = pl.ds(pl.multiple_of(core_index * strip, strip), strip)
    needed = pl.ds(pl.multiple_of(opposite * 2 * depth, 2 * depth), 2 * depth)

    def edge_copy(other):
        return copy(mine.at[strip_rows, needed], ext_mine.at[strip_rows, :], ts.at[7], tr.at[7], other)

    ext_across = copy(ext_mine.at[strip_rows, :], ext_theirs.at[strip_rows, :], ts.at[8], tr.at[8], across)
    ext_core = copy(ext_mine.at[strip_rows, :], ext_mine.at[strip_rows, :], ts.at[9], tr.at[9], core)
    ext_last = copy(ext_theirs.at[strip_rows, :], ext_theirs.at[strip_rows, :], ts.at[10], tr.at[10], core)
    fill = pltpu.make_async_copy(zeros, wgt_all.at[needed, :], loc.at[2])
    pl.when(edge)(lambda: fill.start())
    local = [pltpu.make_async_copy(tok, columns(mine, kv), loc.at[0]),
             pltpu.make_async_copy(
                 wgt.at[y], wgt_all.at[pl.ds(pl.multiple_of(ctx * depth, depth), depth), :], loc.at[1])]
    for c in local:
        c.start()
    def relay_mine():
        own_far.wait_recv()
        mine_core.start()
        own_core.wait_recv()
        mine_core.wait_recv()
        local[0].wait()
        pl.when(z == 0)(lambda: edge_copy(up).start())
        pl.when(z == lines - 1)(lambda: edge_copy(down).start())

    def relay_theirs():
        own_across.wait_recv()
        their_far.start()
        their_core.start()

    def relay_ext():
        @pl.when(inner)
        def _():
            edge_copy(core).wait_recv()
            ext_across.start()
            ext_core.start()

    def travel(d, s):
        for p in range(pieces):
            @pl.when(z >= d)
            def _(p=p):
                up_copy(d - 1, s, p).wait_recv()
                if d < lines - 2:
                    pl.when(has_up)(lambda: up_copy(d, s, p).start())

            @pl.when(z + d < lines)
            def _(p=p):
                down_copy(d - 1, s, p).wait_recv()
                if d < lines - 2:
                    pl.when(has_down)(lambda: down_copy(d, s, p).start())

    travel(1, 0)
    relay_mine()
    relay_theirs()
    for p in range(pieces):
        y_copy(p).wait_recv()
        both_ways(0, 1, p)
    for d in range(2, lines - 1):
        travel(d, 0)
    relay_ext()
    for d in range(1, lines - 1):
        travel(d, 1)

    their_far.wait_recv()
    last_core.start()

    @pl.when(inner)
    def _():
        ext_across.wait_recv()
        ext_last.start()
        ext_core.wait_recv()
        ext_last.wait_recv()
        for c in (ext_across, ext_core, ext_last):
            c.wait_send()

    @pl.when(edge)
    def _():
        edge_copy(core).wait_send()
        fill.wait()

    for c in (their_core, last_core):
        c.wait_recv()
    for c in (own_far, own_core, own_across, mine_core, their_far, their_core, last_core):
        c.wait_send()
    local[1].wait()
    for p in range(pieces):
        y_copy(p).wait_send()
        for s in range(2):
            for d in range(lines - 2):
                pl.when(has_up & (z >= d))(lambda d=d, s=s, p=p: up_copy(d, s, p).wait_send())
                pl.when(has_down & (z + d < lines))(
                    lambda d=d, s=s, p=p: down_copy(d, s, p).wait_send())


def gathered(tokens, weights):
    lines = lax.axis_size("ctx") // 2
    _, depth, width = weights.shape
    pieces = max(1, depth // 256)
    dma = pltpu.SemaphoreType.DMA
    line_sems = [dma((lines, 2, pieces))] * 4
    all_features = jax.ShapeDtypeStruct(
        (tokens.shape[0], tokens.shape[1] * lax.axis_size("kv")), tokens.dtype)
    strip = jax.ShapeDtypeStruct((tokens.shape[0], 2 * depth), tokens.dtype)
    return pl.pallas_call(
        functools.partial(gather_kernel, lines, pieces),
        out_shape=(
            all_features,
            all_features,
            jax.ShapeDtypeStruct((depth * lax.axis_size("ctx"), width), weights.dtype),
            strip,
            strip,
        ),
        in_specs=[pl.BlockSpec(memory_space=pl.ANY)] * 3,
        out_specs=[pl.BlockSpec(memory_space=pl.ANY)] * 5,
        scratch_shapes=[dma((3,)), dma((11,)), dma((11,))] + line_sems + [dma((pieces,))] * 2,
        compiler_params=pltpu.CompilerParams(collective_id=0, has_side_effects=True),
    )(tokens, weights, jnp.zeros((2 * depth, width), weights.dtype))


def shards(tokens, segment_ids, query_weight, key_weight, value_projection_matrix):
    rows = tokens.shape[0]
    wide, half = key_weight.shape[1], query_weight.shape[1] // 2
    packed = jnp.stack([
        jnp.concatenate([key_weight, query_weight[:, :half]], axis=1),
        jnp.concatenate([value_projection_matrix, query_weight[:, half:]], axis=1),
    ])
    mine, theirs, weights, ext_mine, ext_theirs = gathered(tokens, packed)
    length, block = lax.axis_size("ctx"), 2 * query_weight.shape[0]
    pairs = [(i, i ^ 1) for i in range(length)]
    inward = [(2, 0), (3, 1), (length - 4, length - 2), (length - 3, length - 1)]
    begin = jnp.where(lax.axis_index("ctx") // 2 == 1, weights.shape[0] - block, 0)
    opposite = lax.dynamic_slice_in_dim(weights, begin, block, 0)

    def project(whole, matrix):
        return jnp.dot(whole, matrix, preferred_element_type=jnp.float32)

    def help_end(ext):
        return lax.ppermute(project(ext, opposite).astype(jnp.bfloat16), "ctx", inward)

    def finish(own, helped):
        return (own + helped.astype(jnp.float32)).astype(jnp.bfloat16)

    helped_theirs = help_end(ext_theirs)
    own_theirs, ext_mine = lax.optimization_barrier((project(theirs, weights), ext_mine))
    own_theirs, helped_theirs = lax.optimization_barrier((own_theirs, helped_theirs))
    received = lax.ppermute(finish(own_theirs, helped_theirs), "ctx", pairs)
    helped_mine = help_end(ext_mine)
    own_mine, helped_mine, received = lax.optimization_barrier(
        (project(mine, weights), helped_mine, received))
    kept = finish(own_mine, helped_mine)
    first_side = lax.axis_index("ctx") % 2 == 0
    low = jnp.where(first_side, kept, received)
    high = jnp.where(first_side, received, kept)
    key_rows, value_rows = low[:, :wide], high[:, :wide]
    query_rows = jnp.concatenate([low[:, wide:], high[:, wide:]], axis=1)
    prev_key, prev_value = shifted((key_rows, value_rows), "ctx", 1)
    kv_heads = key_weight.shape[1] // HEAD_DIMENSION
    query_group = query_weight.shape[1] // (HEAD_DIMENSION * kv_heads)
    query_matrix = query_rows.reshape(rows, kv_heads, query_group, HEAD_DIMENSION)
    nearby_keys = jnp.concatenate([prev_key, key_rows], axis=0).reshape(
        2 * rows, kv_heads, HEAD_DIMENSION
    )
    nearby_values = jnp.concatenate([prev_value, value_rows], axis=0).reshape(
        2 * rows, kv_heads, HEAD_DIMENSION
    )
    position = lax.axis_index("ctx")
    begin_offset = position * rows
    prev_start = jnp.maximum(begin_offset - rows, 0)
    seg_query = lax.dynamic_slice_in_dim(segment_ids, begin_offset, rows, 0)
    seg_prev = lax.dynamic_slice_in_dim(segment_ids, prev_start, rows, 0)
    seg_keys = jnp.concatenate([seg_prev, seg_query], axis=0)
    qpos = begin_offset + jnp.arange(rows, dtype=jnp.int32)
    kpos = begin_offset - rows + jnp.arange(2 * rows, dtype=jnp.int32)
    visible = (kpos[None, :] <= qpos[:, None]) & (kpos[None, :] > qpos[:, None] - rows)
    visible = visible & (kpos[None, :] >= 0) & (seg_keys[None, :] == seg_query[:, None])
    return attend_block(query_matrix, nearby_keys, nearby_values, visible)


def solution(mesh):
    placed = (P("ctx", "kv"), P(), P("ctx", "kv"), P("ctx", "kv"), P("ctx", "kv"))
    return jax.shard_map(
        shards, mesh=mesh, in_specs=placed, out_specs=P("ctx", "kv"), check_vma=False
    )
```

```python
import functools

import jax
import jax.numpy as jnp
from jax import lax
from jax.experimental import pallas as pl
from jax.experimental.pallas import tpu as pltpu
from jax.sharding import PartitionSpec as P

HEAD_DIMENSION = 128


def shifted(shard, axis, by):
    length = lax.axis_size(axis)
    pairs = [(i, i + by) for i in range(length) if 0 <= i + by < length]
    return lax.ppermute(shard, axis, pairs)


def attend_block(query_matrix, key_matrix, value_matrix, visible):
    head_size = query_matrix.shape[-1]
    scores = jnp.einsum(
        "thgd,shd->hgts", query_matrix, key_matrix, preferred_element_type=jnp.float32
    ) * head_size ** (-0.5)
    scores = jnp.where(visible[None, None], scores, -1e30)
    largest = jnp.max(scores, axis=-1, keepdims=True)
    expon = jnp.where(visible[None, None], jnp.exp(scores - largest), 0.0)
    total = jnp.sum(expon, axis=-1, keepdims=True)
    weights = expon.astype(jnp.bfloat16)
    summed = jnp.einsum("hgts,shd->hgtd", weights, value_matrix, preferred_element_type=jnp.float32)
    result = summed / total
    rows = query_matrix.shape[0]
    return jnp.transpose(result, (2, 0, 1, 3)).reshape(rows, -1).astype(jnp.bfloat16)


MESH = pl.DeviceIdType.MESH


def gather_kernel(lines, pieces, tok, wgt, mine, theirs, wgt_all, loc, ts, tr,
                  up_s, up_r, dn_s, dn_r, y_s, y_r):
    ctx, kv = lax.axis_index("ctx"), lax.axis_index("kv")
    z, y = ctx // 2, ctx % 2
    up, down, across = {"ctx": ctx + 2}, {"ctx": ctx - 2}, {"ctx": z * 2 + (1 - y)}
    other_core, other_chip = (kv // 2) * 2 + (1 - kv % 2), (1 - kv // 2) * 2 + kv % 2
    core, far = {"kv": other_core}, {"kv": other_chip}
    has_up, has_down = z < lines - 1, z > 0
    height, depth, width = tok.shape[1], wgt.shape[0], wgt_all.shape[1]
    rows = depth // pieces

    barrier = pltpu.get_barrier_semaphore()
    for other in (across, core, far):
        pl.semaphore_signal(barrier, inc=1, device_id=other, device_id_type=MESH)

    @pl.when(has_up)
    def _():
        pl.semaphore_signal(barrier, inc=1, device_id=up, device_id_type=MESH)

    @pl.when(has_down)
    def _():
        pl.semaphore_signal(barrier, inc=1, device_id=down, device_id_type=MESH)

    pl.semaphore_wait(barrier, 3 + has_up.astype(jnp.int32) + has_down.astype(jnp.int32))

    def copy(src, dst, send, recv, other):
        return pltpu.make_async_remote_copy(
            src_ref=src, dst_ref=dst, send_sem=send, recv_sem=recv,
            device_id=other, device_id_type=MESH)

    def place(line, side, p):
        start = pl.multiple_of((line * 2 + side) * depth + p * rows, rows)
        return wgt_all.at[pl.ds(start, rows), :]

    def own(half, p):
        return wgt.at[pl.ds(p * rows, rows), pl.ds(pl.multiple_of(half * width, width), width)]

    def block(off, s, p):
        return own(y, p) if (off, s) == (0, 0) else place(z + off, y if s == 0 else 1 - y, p)

    def up_copy(d, s, p):
        dst = place(z - d, y if s == 0 else 1 - y, p)
        return copy(block(-d, s, p), dst, up_s.at[d, s, p], up_r.at[d, s, p], up)

    def down_copy(d, s, p):
        dst = place(z + d, y if s == 0 else 1 - y, p)
        return copy(block(d, s, p), dst, dn_s.at[d, s, p], dn_r.at[d, s, p], down)

    def y_copy(p):
        return copy(own(1 - y, p), place(z, y, p), y_s.at[p], y_r.at[p], across)

    def columns(ref, k):
        return ref.at[:, pl.ds(pl.multiple_of(k * height, height), height)]

    def both_ways(d, s, p):
        pl.when(has_up)(lambda: up_copy(d, s, p).start())
        pl.when(has_down)(lambda: down_copy(d, s, p).start())

    own_far = copy(tok, columns(mine, kv), ts.at[0], tr.at[0], far)
    own_core = copy(tok, columns(mine, kv), ts.at[1], tr.at[1], core)
    own_across = copy(tok, columns(theirs, kv), ts.at[2], tr.at[2], across)
    mine_core = copy(columns(mine, other_chip), columns(mine, other_chip), ts.at[3], tr.at[3], core)
    their_far = copy(columns(theirs, kv), columns(theirs, kv), ts.at[4], tr.at[4], far)
    their_core = copy(columns(theirs, kv), columns(theirs, kv), ts.at[5], tr.at[5], core)
    last_core = copy(columns(theirs, other_chip), columns(theirs, other_chip), ts.at[6], tr.at[6], core)

    for p in range(pieces):
        y_copy(p).start()
        both_ways(0, 0, p)
    own_far.start()
    own_across.start()
    own_core.start()
    local = [pltpu.make_async_copy(tok, columns(mine, kv), loc.at[0]),
             pltpu.make_async_copy(
                 wgt.at[:, pl.ds(pl.multiple_of(y * width, width), width)],
                 wgt_all.at[pl.ds(pl.multiple_of(ctx * depth, depth), depth), :], loc.at[1])]
    for c in local:
        c.start()
    for p in range(pieces):
        y_copy(p).wait_recv()
        both_ways(0, 1, p)

    def relay_mine():
        own_far.wait_recv()
        mine_core.start()

    def relay_theirs():
        own_across.wait_recv()
        their_far.start()
        their_core.start()

    def relay_last():
        their_far.wait_recv()
        last_core.start()

    relays = {(1, 1): relay_mine, (2, 0): relay_theirs, (3, 0): relay_last}
    for d in range(1, lines):
        for s in range(2):
            for p in range(pieces):
                @pl.when(z >= d)
                def _(d=d, s=s, p=p):
                    up_copy(d - 1, s, p).wait_recv()
                    if d < lines - 1:
                        pl.when(has_up)(lambda: up_copy(d, s, p).start())

                @pl.when(z + d < lines)
                def _(d=d, s=s, p=p):
                    down_copy(d - 1, s, p).wait_recv()
                    if d < lines - 1:
                        pl.when(has_down)(lambda: down_copy(d, s, p).start())
            if (d, s) in relays:
                relays.pop((d, s))()
    for key in sorted(relays):
        relays[key]()

    for c in (own_core, mine_core, their_core, last_core):
        c.wait_recv()
    for c in (own_far, own_core, own_across, mine_core, their_far, their_core, last_core):
        c.wait_send()
    for c in local:
        c.wait()
    for p in range(pieces):
        y_copy(p).wait_send()
        for s in range(2):
            for d in range(lines - 1):
                pl.when(has_up & (z >= d))(lambda d=d, s=s, p=p: up_copy(d, s, p).wait_send())
                pl.when(has_down & (z + d < lines))(
                    lambda d=d, s=s, p=p: down_copy(d, s, p).wait_send())


def gathered(tokens, weights):
    lines = lax.axis_size("ctx") // 2
    depth, width = weights.shape[0], weights.shape[1] // 2
    pieces = max(1, depth // 256)
    dma = pltpu.SemaphoreType.DMA
    line_sems = [dma((lines, 2, pieces))] * 4
    all_features = jax.ShapeDtypeStruct(
        (tokens.shape[0], tokens.shape[1] * lax.axis_size("kv")), tokens.dtype)
    return pl.pallas_call(
        functools.partial(gather_kernel, lines, pieces),
        out_shape=(
            all_features,
            all_features,
            jax.ShapeDtypeStruct((depth * lax.axis_size("ctx"), width), weights.dtype),
        ),
        in_specs=[pl.BlockSpec(memory_space=pl.ANY)] * 2,
        out_specs=[pl.BlockSpec(memory_space=pl.ANY)] * 3,
        scratch_shapes=[dma((2,)), dma((7,)), dma((7,))] + line_sems + [dma((pieces,))] * 2,
        compiler_params=pltpu.CompilerParams(collective_id=0, has_side_effects=True),
    )(tokens, weights)


def shards(tokens, segment_ids, query_weight, key_weight, value_projection_matrix):
    rows = tokens.shape[0]
    wide, half = key_weight.shape[1], query_weight.shape[1] // 2
    packed = jnp.concatenate(
        [key_weight, query_weight[:, :half], value_projection_matrix, query_weight[:, half:]], axis=1)
    mine, theirs, weights = gathered(tokens, packed)

    def project(whole):
        return jnp.dot(whole, weights, preferred_element_type=jnp.float32).astype(jnp.bfloat16)

    pairs = [(i, i ^ 1) for i in range(lax.axis_size("ctx"))]
    received = lax.ppermute(project(theirs), "ctx", pairs)
    kept, received = lax.optimization_barrier((project(mine), received))
    first_side = lax.axis_index("ctx") % 2 == 0
    low = jnp.where(first_side, kept, received)
    high = jnp.where(first_side, received, kept)
    key_rows, value_rows = low[:, :wide], high[:, :wide]
    query_rows = jnp.concatenate([low[:, wide:], high[:, wide:]], axis=1)
    previous = shifted(jnp.concatenate([key_rows, value_rows], axis=1), "ctx", 1)
    prev_key, prev_value = previous[:, :wide], previous[:, wide:]
    kv_heads = key_weight.shape[1] // HEAD_DIMENSION
    query_group = query_weight.shape[1] // (HEAD_DIMENSION * kv_heads)
    query_matrix = query_rows.reshape(rows, kv_heads, query_group, HEAD_DIMENSION)
    nearby_keys = jnp.concatenate([prev_key, key_rows], axis=0).reshape(
        2 * rows, kv_heads, HEAD_DIMENSION
    )
    nearby_values = jnp.concatenate([prev_value, value_rows], axis=0).reshape(
        2 * rows, kv_heads, HEAD_DIMENSION
    )
    position = lax.axis_index("ctx")
    begin_offset = position * rows
    prev_start = jnp.maximum(begin_offset - rows, 0)
    seg_query = lax.dynamic_slice_in_dim(segment_ids, begin_offset, rows, 0)
    seg_prev = lax.dynamic_slice_in_dim(segment_ids, prev_start, rows, 0)
    seg_keys = jnp.concatenate([seg_prev, seg_query], axis=0)
    qpos = begin_offset + jnp.arange(rows, dtype=jnp.int32)
    kpos = begin_offset - rows + jnp.arange(2 * rows, dtype=jnp.int32)
    visible = (kpos[None, :] <= qpos[:, None]) & (kpos[None, :] > qpos[:, None] - rows)
    visible = visible & (kpos[None, :] >= 0) & (seg_keys[None, :] == seg_query[:, None])
    return attend_block(query_matrix, nearby_keys, nearby_values, visible)


def solution(mesh):
    placed = (P("ctx", "kv"), P(), P("ctx", "kv"), P("ctx", "kv"), P("ctx", "kv"))
    return jax.shard_map(
        shards, mesh=mesh, in_specs=placed, out_specs=P("ctx", "kv"), check_vma=False
    )
```
